512 devices in a mesh: layer: 16 (over z_lo, y), ex: 32 (over x, z_hi, core).
Axes of the slice: x: 4, y: 4, z: 16 (z_hi: 4, z_lo: 4; z = z_hi * 4 + z_lo), core: 2. Of those that a mesh axis runs over, the one named last changes fastest.
Arguments:
- train_grads: bfloat16 [16, 16384, 2048], P('layer', 'ex'), may hold values from -0.03125 to 0.03125
- query_grads: bfloat16 [16, 1024, 2048], P('layer', 'ex'), may hold values from -6 to 6
- inverse_fisher: bfloat16 [16, 2048, 2048], P('layer', 'ex'), may hold values from -1 to 6, as said below
Outputs:
- scores: float32 [16384, 1024], P('ex', 'layer')
The draws below stay inside these ranges and needn't reach their ends.
Inputs may be any that keep to these rules, and one draw needn't show every extreme that they name: `inverse_fisher`: each layer's block is exactly symmetric.
All inputs are finite; a program needn't handle non-finite values.
Results may differ from the reference program's by a relative error of at most 0.0029.
Values may be sent and summed in bfloat16 or wider, within the bound.
No kernel may reach another device: no remote copies, remote signals or barrier semaphores. Data moves between devices by JAX's collectives and lax.ppermute only.
A program may use at most 64 MiB of HBM per device.

```python
import math
import jax
import jax.numpy as jnp
from jax import lax

K = 2048
LAYERS = 16
TRAIN = 16384
QUERIES = 1024


def draw_inverse_fisher(key, part):
    key = jax.random.fold_in(key, 7)
    first_key, second_key = jax.random.split(key)
    noise = jax.random.normal(first_key, (LAYERS, K, K), jnp.float32)
    symmetric = (noise + jnp.swapaxes(noise, 1, 2)) * (0.35 / math.sqrt(K))
    log_diag = jax.random.uniform(second_key, (LAYERS, K), jnp.float32, math.log(0.5), math.log(2.0))
    identity = jnp.eye(K, dtype=jnp.float32)
    return (symmetric + identity[None, :, :] * jnp.exp(log_diag)[:, :, None]).astype(jnp.bfloat16)


def block_scale(rng, dims, pieces, least, high):
    level, own = 1.0, jax.random.fold_in(rng, 6)
    for dim, parts in pieces:
        draws = jnp.exp(jax.random.uniform(jax.random.fold_in(own, dim), (parts,), jnp.float32, least / len(pieces), high / len(pieces)))
        level = level * jnp.repeat(draws, dims[dim] // parts).reshape([-1 if axis == dim else 1 for axis in range(len(dims))])
    return level


def bell_draw(stream_key, extent, spread, most, pieces=(), kind=jnp.bfloat16):
    entries = jax.random.normal(stream_key, extent, jnp.float32) * spread
    if len(pieces) > 0:
        entries = block_scale(stream_key, extent, pieces, -0.22, 0.18) * entries
    return jnp.clip(entries, min=-most, max=most).astype(kind)


def setup_inputs(seed: int = 0) -> dict:
    streams_of = jax.random.split(jax.random.key(seed), 4)
    train_grads = bell_draw(streams_of[0], (LAYERS, TRAIN, K), (K * LAYERS) ** -0.5, 0.03125, ((0, 16), (1, 32)))
    query_grads = bell_draw(streams_of[1], (LAYERS, QUERIES, K), 1.0, 6.0, ((0, 16), (1, 32)))
    inverse_fisher = draw_inverse_fisher(jax.random.fold_in(streams_of[3], 71), 0)
    return dict(train_grads=train_grads, query_grads=query_grads, inverse_fisher=inverse_fisher)


def reference(train_grads, query_grads, inverse_fisher):
    def one_layer(summed, layer_idx):
        conditioned = jnp.dot(query_grads[layer_idx], inverse_fisher[layer_idx], preferred_element_type=jnp.float32).astype(jnp.bfloat16)
        layer_scores = jnp.dot(train_grads[layer_idx], conditioned.T, preferred_element_type=jnp.float32)
        return summed + layer_scores, None

    initial = jnp.zeros((train_grads.shape[1], query_grads.shape[1]), jnp.float32)
    summed, unused = lax.scan(one_layer, initial, jnp.arange(train_grads.shape[0], dtype=jnp.int32))
    return summed
```

```python
import jax
import jax.numpy as jnp
from jax import lax
from jax.sharding import Mesh
from jax.sharding import PartitionSpec as P

LAYER = ("zl", "y")
EX = ("x", "zh", "c")


def copies(block, n):
    return jnp.broadcast_to(block[None], (n,) + block.shape)


def on_device(train_grads, query_grads, inverse_fisher):
    train, query, fisher = train_grads[0], query_grads[0], inverse_fisher[0]
    rows, k = train.shape
    plane = lax.all_to_all(copies(fisher, 8), ("x", "c"), 0, 0)
    plane = plane.reshape(-1, k)
    ordered = train.reshape(rows, 4, 4, k // 16).swapaxes(1, 2).reshape(rows, k)
    pair = lax.all_gather(ordered, "c", axis=0, tiled=True)
    queries = lax.all_gather(query, "zh", axis=0, tiled=True)
    conditioned = lax.dot_general(
        queries, plane, (((1,), (1,)), ((), ())), preferred_element_type=jnp.float32
    ).astype(jnp.bfloat16)
    conditioned = lax.all_gather(conditioned, "zh", axis=1, tiled=True)
    conditioned = lax.all_to_all(copies(conditioned, 4), "x", 0, 0).reshape(-1, k)
    part = lax.dot_general(
        conditioned, pair, (((1,), (1,)), ((), ())), preferred_element_type=jnp.float32
    ).astype(jnp.bfloat16)
    part = part.reshape(16, -1, 2, rows).swapaxes(1, 2).reshape(32, -1, rows)
    part = lax.all_to_all(part, LAYER + ("c",), 0, 0)
    total = part.reshape(16, -1, rows).astype(jnp.float32).sum(axis=0)
    return total.T


def solution(mesh):
    split = Mesh(mesh.devices.reshape(4, 4, 4, 4, 2), LAYER + EX)
    spec = P(LAYER, EX, None)
    return jax.shard_map(
        on_device,
        mesh=split,
        in_specs=(spec, spec, spec),
        out_specs=P(EX, LAYER),
        check_vma=False,
    )
```

```python
import jax
import jax.numpy as jnp
from jax import lax
from jax.sharding import Mesh
from jax.sharding import PartitionSpec as P

LAYER = ("zl", "y")
EX = ("x", "zh", "c")
SWAP = [(0, 1), (1, 0)]


def copies(block, n):
    return jnp.broadcast_to(block[None], (n,) + block.shape)


def rows_by_rows(a, b):
    return lax.dot_general(
        a, b, (((1,), (1,)), ((), ())), preferred_element_type=jnp.float32
    ).astype(jnp.bfloat16)


def on_device(train_grads, query_grads, inverse_fisher):
    train, query, fisher = train_grads[0], query_grads[0], inverse_fisher[0]
    rows, k = train.shape
    plane = lax.all_to_all(copies(fisher, 8), ("x", "c"), 0, 0)
    plane = plane.reshape(-1, k)
    other = lax.ppermute(train, "c", SWAP)
    queries = lax.all_gather(query, "zh", axis=0, tiled=True)
    conditioned = rows_by_rows(queries, plane)
    conditioned = lax.all_gather(conditioned, "zh", axis=0)
    conditioned = conditioned.reshape(4, -1, 4, k // 16).transpose(1, 2, 0, 3)
    conditioned = conditioned.reshape(-1, k)
    conditioned = lax.all_to_all(copies(conditioned, 4), "x", 0, 0).reshape(-1, k)
    own, far = rows_by_rows(conditioned, train), rows_by_rows(conditioned, other)
    own, far = own.reshape(16, -1, rows), far.reshape(16, -1, rows)
    first = lax.axis_index("c") == 0
    part = jnp.stack([jnp.where(first, own, far), jnp.where(first, far, own)], axis=1)
    part = lax.all_to_all(part.reshape(32, -1, rows), LAYER + ("c",), 0, 0)
    total = part.reshape(16, -1, rows).astype(jnp.float32).sum(axis=0)
    return total.T


def solution(mesh):
    split = Mesh(mesh.devices.reshape(4, 4, 4, 4, 2), LAYER + EX)
    spec = P(LAYER, EX, None)
    return jax.shard_map(
        on_device,
        mesh=split,
        in_specs=(spec, spec, spec),
        out_specs=P(EX, LAYER),
        check_vma=False,
    )
```

```python
import jax
import jax.numpy as jnp
from jax import lax
from jax.experimental import pallas as pl
from jax.experimental.pallas import tpu as pltpu
from jax.sharding import Mesh
from jax.sharding import PartitionSpec as P

LAYER = ("zl", "y")
EX = ("x", "zh", "c")
SWAP = [(0, 1), (1, 0)]


def copies(block, n):
    return jnp.broadcast_to(block[None], (n,) + block.shape)


def spread(block_ref, out_ref, sem):
    sent = [pltpu.make_async_copy(block_ref, out_ref.at[n], sem.at[n]) for n in range(8)]
    for copy in sent:
        copy.start()
    for copy in sent:
        copy.wait()


def rows_by_rows(a, b):
    return lax.dot_general(
        a, b, (((1,), (1,)), ((), ())), preferred_element_type=jnp.float32
    )


def condition(query_ref, plane_hbm, out_ref, plane, sems):
    arriving = [
        pltpu.make_async_copy(plane_hbm.at[x], plane.at[x], sems.at[x]) for x in range(4)
    ]
    for copy in arriving:
        copy.start()
    for x in range(4):
        arriving[x].wait()
        out = rows_by_rows(query_ref[...], plane[x])
        out_ref[:, x * 128 : x * 128 + 128] = out.astype(jnp.bfloat16)


def score(conditioned_ref, near_ref, far_hbm, out_ref, far_ref, sem):
    core = lax.axis_index("c")
    rows, k = near_ref.shape
    wide, thin = k // 4, k // 16
    arriving = pltpu.make_async_copy(far_hbm, far_ref, sem)
    arriving.start()
    for side, train_ref in enumerate((near_ref, far_ref)):
        if side == 1:
            arriving.wait()
        owner = core if side == 0 else 1 - core
        for at in range(0, rows, 256):
            train = train_ref[at : at + 256, :]
            total = jnp.zeros((512, 256), jnp.float32)
            for z in range(4):
                columns = [train[:, (x * 4 + z) * thin :][:, :thin] for x in range(4)]
                total += rows_by_rows(
                    conditioned_ref[:, z].reshape(-1, wide), jnp.concatenate(columns, axis=1)
                )
            out_ref[:, owner, :, at : at + 256] = total.astype(jnp.bfloat16).reshape(16, -1, 256)


def on_device(train_grads, query_grads, inverse_fisher):
    train, query, fisher = train_grads[0], query_grads[0], inverse_fisher[0]
    rows, k = train.shape
    mine = query.shape[0]
    eight = pl.pallas_call(
        spread,
        out_shape=jax.ShapeDtypeStruct((8,) + fisher.shape, fisher.dtype),
        in_specs=[pl.BlockSpec(memory_space=pltpu.VMEM)],
        out_specs=pl.BlockSpec(memory_space=pl.ANY),
        scratch_shapes=[pltpu.SemaphoreType.DMA((8,))],
        name="spread",
    )(fisher)
    plane = lax.all_to_all(eight, ("x", "c"), 0, 0)
    plane = plane.reshape(4, -1, k)
    far = lax.ppermute(train, "c", SWAP)
    queries = lax.all_gather(query, "zh", axis=0, tiled=True)
    conditioned = pl.pallas_call(
        condition,
        out_shape=jax.ShapeDtypeStruct((4 * mine, k // 4), jnp.bfloat16),
        in_specs=[pl.BlockSpec(memory_space=pltpu.VMEM), pl.BlockSpec(memory_space=pl.ANY)],
        scratch_shapes=[pltpu.VMEM(plane.shape, jnp.bfloat16), pltpu.SemaphoreType.DMA((4,))],
        compiler_params=pltpu.CompilerParams(vmem_limit_bytes=14 * 2**20),
        cost_estimate=pl.CostEstimate(
            flops=2 * mine * k * k, bytes_accessed=3 * 2**20, transcendentals=0
        ),
        name="condition",
    )(queries, plane)
    conditioned = lax.all_gather(conditioned, "zh", axis=0)
    conditioned, far = lax.optimization_barrier((conditioned, far))
    conditioned = lax.all_to_all(copies(conditioned, 4), "x", 0, 0)
    part = pl.pallas_call(
        score,
        out_shape=jax.ShapeDtypeStruct((16, 2, mine, rows), jnp.bfloat16),
        in_specs=[pl.BlockSpec(memory_space=pltpu.VMEM)] * 2 + [pl.BlockSpec(memory_space=pl.ANY)],
        scratch_shapes=[pltpu.VMEM((rows, k), jnp.bfloat16), pltpu.SemaphoreType.DMA],
        compiler_params=pltpu.CompilerParams(vmem_limit_bytes=14 * 2**20),
        cost_estimate=pl.CostEstimate(
            flops=4 * 16 * mine * rows * k, bytes_accessed=8 * 2**20, transcendentals=0
        ),
        name="score",
    )(conditioned, train, far)
    part = lax.all_to_all(part.reshape(32, mine, rows), LAYER + ("c",), 0, 0)
    total = part.reshape(16, -1, rows).astype(jnp.float32).sum(axis=0)
    return total.T


def solution(mesh):
    split = Mesh(mesh.devices.reshape(4, 4, 4, 4, 2), LAYER + EX)
    spec = P(LAYER, EX, None)
    return jax.shard_map(
        on_device,
        mesh=split,
        in_specs=(spec, spec, spec),
        out_specs=P(EX, LAYER),
        check_vma=False,
    )
```

```python
import jax
import jax.numpy as jnp
from jax import lax
from jax.experimental import pallas as pl
from jax.experimental.pallas import tpu as pltpu
from jax.sharding import Mesh
from jax.sharding import PartitionSpec as P

LAYER = ("z1", "z0", "y")
EX = ("x", "zh", "c")
SWAP = [(0, 1), (1, 0)]


def copies(block, n):
    return jnp.broadcast_to(block[None], (n,) + block.shape)


def spread(block_ref, out_ref, sem):
    sent = [pltpu.make_async_copy(block_ref, out_ref.at[n], sem.at[n]) for n in range(8)]
    for copy in sent:
        copy.start()
    for copy in sent:
        copy.wait()


def rows_by_rows(a, b):
    return lax.dot_general(
        a, b, (((1,), (1,)), ((), ())), preferred_element_type=jnp.float32
    )


def condition(query_ref, plane_hbm, out_ref, plane, sems):
    arriving = [
        pltpu.make_async_copy(plane_hbm.at[x], plane.at[x], sems.at[x]) for x in range(4)
    ]
    for copy in arriving:
        copy.start()
    for x in range(4):
        arriving[x].wait()
        out = rows_by_rows(query_ref[...], plane[x])
        out_ref[:, x * 128 : x * 128 + 128] = out.astype(jnp.bfloat16)


def score(conditioned_ref, near_ref, far_hbm, out_ref, far_ref, sem):
    core = lax.axis_index("c")
    rows, k = near_ref.shape
    wide, thin = k // 4, k // 16
    arriving = pltpu.make_async_copy(far_hbm, far_ref, sem)
    arriving.start()
    for side, train_ref in enumerate((near_ref, far_ref)):
        if side == 1:
            arriving.wait()
        owner = core if side == 0 else 1 - core
        for at in range(0, rows, 256):
            train = train_ref[at : at + 256, :]
            total = jnp.zeros((512, 256), jnp.float32)
            for z in range(4):
                columns = [train[:, (x * 4 + z) * thin :][:, :thin] for x in range(4)]
                total += rows_by_rows(
                    conditioned_ref[:, z].reshape(-1, wide), jnp.concatenate(columns, axis=1)
                )
            total = total.astype(jnp.bfloat16).reshape(2, 2, 4, -1, 256)
            for z1 in range(2):
                out_ref[:, :, owner, z1, :, at : at + 256] = total[z1]


def sum_layers(part_ref, keep_ref, send_ref):
    mine = lax.axis_index("z1")
    for side in range(2):
        for out_ref, z1 in ((keep_ref, mine), (send_ref, 1 - mine)):
            total = part_ref[0, side, z1].astype(jnp.float32)
            for n in range(1, 8):
                total += part_ref[n, side, z1].astype(jnp.float32)
            out_ref[side] = total.astype(out_ref.dtype)


def on_device(train_grads, query_grads, inverse_fisher):
    train, query, fisher = train_grads[0], query_grads[0], inverse_fisher[0]
    rows, k = train.shape
    mine = query.shape[0]
    eight = pl.pallas_call(
        spread,
        out_shape=jax.ShapeDtypeStruct((8,) + fisher.shape, fisher.dtype),
        in_specs=[pl.BlockSpec(memory_space=pltpu.VMEM)],
        out_specs=pl.BlockSpec(memory_space=pl.ANY),
        scratch_shapes=[pltpu.SemaphoreType.DMA((8,))],
        name="spread",
    )(fisher)
    plane = lax.all_to_all(eight, ("x", "c"), 0, 0)
    plane = plane.reshape(4, -1, k)
    far = lax.ppermute(train, "c", SWAP)
    queries = lax.all_gather(query, "zh", axis=0, tiled=True)
    conditioned = pl.pallas_call(
        condition,
        out_shape=jax.ShapeDtypeStruct((4 * mine, k // 4), jnp.bfloat16),
        in_specs=[pl.BlockSpec(memory_space=pltpu.VMEM), pl.BlockSpec(memory_space=pl.ANY)],
        scratch_shapes=[pltpu.VMEM(plane.shape, jnp.bfloat16), pltpu.SemaphoreType.DMA((4,))],
        compiler_params=pltpu.CompilerParams(vmem_limit_bytes=14 * 2**20),
        cost_estimate=pl.CostEstimate(
            flops=2 * mine * k * k, bytes_accessed=3 * 2**20, transcendentals=0
        ),
        name="condition",
    )(queries, plane)
    conditioned = lax.all_gather(conditioned, "zh", axis=0)
    conditioned, far = lax.optimization_barrier((conditioned, far))
    conditioned = lax.all_to_all(copies(conditioned, 4), "x", 0, 0)
    part = pl.pallas_call(
        score,
        out_shape=jax.ShapeDtypeStruct((2, 4, 2, 2, mine, rows), jnp.bfloat16),
        in_specs=[pl.BlockSpec(memory_space=pltpu.VMEM)] * 2 + [pl.BlockSpec(memory_space=pl.ANY)],
        scratch_shapes=[pltpu.VMEM((rows, k), jnp.bfloat16), pltpu.SemaphoreType.DMA],
        compiler_params=pltpu.CompilerParams(vmem_limit_bytes=14 * 2**20),
        cost_estimate=pl.CostEstimate(
            flops=4 * 16 * mine * rows * k, bytes_accessed=8 * 2**20, transcendentals=0
        ),
        name="score",
    )(conditioned, train, far)
    part = lax.all_to_all(part.reshape(16, 2, mine, rows), ("z0", "y", "c"), 0, 0)
    keep, send = pl.pallas_call(
        sum_layers,
        out_shape=(
            jax.ShapeDtypeStruct((2, mine, rows), jnp.float32),
            jax.ShapeDtypeStruct((2, mine, rows), jnp.bfloat16),
        ),
        compiler_params=pltpu.CompilerParams(vmem_limit_bytes=14 * 2**20),
        name="sum_layers",
    )(part.reshape(8, 2, 2, mine, rows))
    total = keep + lax.ppermute(send, "z1", SWAP).astype(jnp.float32)
    return total.reshape(2 * mine, rows).T


def solution(mesh):
    split = Mesh(mesh.devices.reshape(2, 2, 4, 4, 4, 2), LAYER + EX)
    spec = P(LAYER, EX, None)
    return jax.shard_map(
        on_device,
        mesh=split,
        in_specs=(spec, spec, spec),
        out_specs=P(EX, LAYER),
        check_vma=False,
    )
```

```python
import jax
import jax.numpy as jnp
from jax import lax
from jax.experimental import pallas as pl
from jax.experimental.pallas import tpu as pltpu
from jax.sharding import Mesh
from jax.sharding import PartitionSpec as P

LAYER = ("z1", "z0", "y")
EX = ("x", "zh", "c")
SWAP = [(0, 1), (1, 0)]


def copies(block, n):
    return jnp.broadcast_to(block[None], (n,) + block.shape)


def spread(block_ref, out_ref, sem):
    sent = [pltpu.make_async_copy(block_ref, out_ref.at[n], sem.at[n]) for n in range(8)]
    for copy in sent:
        copy.start()
    for copy in sent:
        copy.wait()


def rows_by_rows(a, b):
    return lax.dot_general(
        a, b, (((1,), (1,)), ((), ())), preferred_element_type=jnp.float32
    )


def condition(query_ref, plane_ref, out_ref):
    for x in range(4):
        out = rows_by_rows(query_ref[...], plane_ref[x])
        out_ref[:, x * 128 : x * 128 + 128] = out.astype(jnp.bfloat16)


def score(conditioned_ref, near_ref, far_hbm, out_ref, far_ref, sem):
    core = lax.axis_index("c")
    rows, k = near_ref.shape
    wide, thin = k // 4, k // 16
    arriving = pltpu.make_async_copy(far_hbm, far_ref, sem)
    arriving.start()
    for side, train_ref in enumerate((near_ref, far_ref)):
        if side == 1:
            arriving.wait()
        owner = core if side == 0 else 1 - core
        for at in range(0, rows, 256):
            train = train_ref[at : at + 256, :]
            total = jnp.zeros((512, 256), jnp.float32)
            for z in range(4):
                columns = [train[:, (x * 4 + z) * thin :][:, :thin] for x in range(4)]
                total += rows_by_rows(
                    conditioned_ref[:, z].reshape(-1, wide), jnp.concatenate(columns, axis=1)
                )
            total = total.astype(jnp.bfloat16).reshape(2, 2, 4, -1, 256)
            for z1 in range(2):
                out_ref[:, :, owner, z1, :, at : at + 256] = total[z1]


def sum_layers(part_ref, keep_ref, send_ref):
    mine = lax.axis_index("z1")
    for side in range(2):
        for out_ref, z1 in ((keep_ref, mine), (send_ref, 1 - mine)):
            total = part_ref[0, side, z1].astype(jnp.float32)
            for n in range(1, 8):
                total += part_ref[n, side, z1].astype(jnp.float32)
            out_ref[side] = total.astype(out_ref.dtype)


def on_device(train_grads, query_grads, inverse_fisher):
    train, query, fisher = train_grads[0], query_grads[0], inverse_fisher[0]
    rows, k = train.shape
    mine = query.shape[0]
    eight = pl.pallas_call(
        spread,
        out_shape=jax.ShapeDtypeStruct((8,) + fisher.shape, fisher.dtype),
        in_specs=[pl.BlockSpec(memory_space=pltpu.VMEM)],
        out_specs=pl.BlockSpec(memory_space=pl.ANY),
        scratch_shapes=[pltpu.SemaphoreType.DMA((8,))],
        name="spread",
    )(fisher)
    plane = lax.all_to_all(eight, ("x", "c"), 0, 0)
    plane = plane.reshape(4, -1, k)
    far = lax.ppermute(train, "c", SWAP)
    queries = lax.all_gather(query, "zh", axis=0, tiled=True)
    conditioned = pl.pallas_call(
        condition,
        out_shape=jax.ShapeDtypeStruct((4 * mine, k // 4), jnp.bfloat16),
                compiler_params=pltpu.CompilerParams(vmem_limit_bytes=14 * 2**20),
        cost_estimate=pl.CostEstimate(
            flops=2 * mine * k * k, bytes_accessed=3 * 2**20, transcendentals=0
        ),
        name="condition",
    )(queries, plane)
    conditioned = lax.all_gather(conditioned, "zh", axis=0)
    conditioned, far = lax.optimization_barrier((conditioned, far))
    conditioned = lax.all_to_all(copies(conditioned, 4), "x", 0, 0)
    part = pl.pallas_call(
        score,
        out_shape=jax.ShapeDtypeStruct((2, 4, 2, 2, mine, rows), jnp.bfloat16),
        in_specs=[pl.BlockSpec(memory_space=pltpu.VMEM)] * 2 + [pl.BlockSpec(memory_space=pl.ANY)],
        scratch_shapes=[pltpu.VMEM((rows, k), jnp.bfloat16), pltpu.SemaphoreType.DMA],
        compiler_params=pltpu.CompilerParams(vmem_limit_bytes=14 * 2**20),
        cost_estimate=pl.CostEstimate(
            flops=4 * 16 * mine * rows * k, bytes_accessed=8 * 2**20, transcendentals=0
        ),
        name="score",
    )(conditioned, train, far)
    part = lax.all_to_all(part.reshape(16, 2, mine, rows), ("z0", "y", "c"), 0, 0)
    keep, send = pl.pallas_call(
        sum_layers,
        out_shape=(
            jax.ShapeDtypeStruct((2, mine, rows), jnp.float32),
            jax.ShapeDtypeStruct((2, mine, rows), jnp.bfloat16),
        ),
        compiler_params=pltpu.CompilerParams(vmem_limit_bytes=14 * 2**20),
        name="sum_layers",
    )(part.reshape(8, 2, 2, mine, rows))
    total = keep + lax.ppermute(send, "z1", SWAP).astype(jnp.float32)
    return total.reshape(2 * mine, rows).T


def solution(mesh):
    split = Mesh(mesh.devices.reshape(2, 2, 4, 4, 4, 2), LAYER + EX)
    spec = P(LAYER, EX, None)
    return jax.shard_map(
        on_device,
        mesh=split,
        in_specs=(spec, spec, spec),
        out_specs=P(EX, LAYER),
        check_vma=False,
    )
```

```python
import jax
import jax.numpy as jnp
from jax import lax
from jax.experimental import pallas as pl
from jax.experimental.pallas import tpu as pltpu
from jax.sharding import Mesh
from jax.sharding import PartitionSpec as P

LAYER = ("z1", "z0", "y")
EX = ("x", "zh", "c")
SWAP = [(0, 1), (1, 0)]


def copies(block, n):
    return jnp.broadcast_to(block[None], (n,) + block.shape)


def spread(block_ref, out_ref, sem):
    sent = [pltpu.make_async_copy(block_ref, out_ref.at[n], sem.at[n]) for n in range(8)]
    for copy in sent:
        copy.start()
    for copy in sent:
        copy.wait()


def rows_by_rows(a, b):
    return lax.dot_general(
        a, b, (((1,), (1,)), ((), ())), preferred_element_type=jnp.float32
    )


def condition(query_ref, plane_ref, out_ref):
    for x in range(4):
        out = rows_by_rows(query_ref[...], plane_ref[x])
        out_ref[:, x * 128 : x * 128 + 128] = out.astype(jnp.bfloat16)


OWN = ((0, 0), (0, 1))
SIDES = ((3, 0), (1, 1), (3, 1), (1, 0))
OPPOSITE = ((2, 0), (2, 1))


def shift_x(block, by):
    return lax.ppermute(block, "x", [(i, (i + by) % 4) for i in range(4)])


def score(halves, trains, put, arrived=None):
    core = lax.axis_index("c")
    rows, k = trains[0].shape
    thin = k // 16
    for side, train_ref in enumerate(trains):
        if side == 1 and arrived is not None:
            arrived.wait()
        owner = core if side == 0 else 1 - core
        for at in range(0, rows, 256):
            train = train_ref[at : at + 256, :]
            total = None
            for z in range(4):
                columns = [train[:, (x * 4 + z) * thin :][:, :thin] for x in range(4)]
                part = rows_by_rows(
                    jnp.concatenate([half[z] for half in halves], axis=0),
                    jnp.concatenate(columns, axis=1),
                )
                total = part if total is None else total + part
            put(owner, at, total.astype(jnp.bfloat16).reshape(len(halves), 2, -1, 256))


def score_own(first_ref, second_ref, near_ref, far_hbm, out_ref, far_ref, sem):
    arriving = pltpu.make_async_copy(far_hbm, far_ref, sem)
    arriving.start()

    def put(owner, at, block):
        out_ref[:, :, owner, :, at : at + 256] = block

    score((first_ref, second_ref), (near_ref, far_ref), put, arriving)


def score_sides(*refs):
    out_ref = refs[-1]

    def put(owner, at, block):
        out_ref[:, :, owner, :, at : at + 256] = block

    score(refs[:4], refs[4:6], put)


def score_last(first_ref, second_ref, near_ref, far_ref, own_ref, sides_ref, out_ref):
    x = lax.axis_index("x")
    for order, scored in ((OWN, own_ref), (SIDES, sides_ref)):
        for n, (step, half) in enumerate(order):
            at = lax.rem(x + step, 4)
            out_ref[lax.rem(at, 2), 2 * half : 2 * half + 2, :, at // 2] = scored[n]

    def put(owner, at, block):
        to = lax.rem(x + 2, 4)
        for n, (_, half) in enumerate(OPPOSITE):
            out_ref[lax.rem(to, 2), 2 * half : 2 * half + 2, owner, to // 2, :, at : at + 256] = block[n]

    score((first_ref, second_ref), (near_ref, far_ref), put)


def sum_layers(part_ref, keep_ref, send_ref):
    mine = lax.axis_index("z1")
    for side in range(2):
        for out_ref, z1 in ((keep_ref, mine), (send_ref, 1 - mine)):
            total = part_ref[0, side, z1].astype(jnp.float32)
            for n in range(1, 8):
                total += part_ref[n, side, z1].astype(jnp.float32)
            out_ref[side] = total.astype(out_ref.dtype)


def on_device(train_grads, query_grads, inverse_fisher):
    train, query, fisher = train_grads[0], query_grads[0], inverse_fisher[0]
    rows, k = train.shape
    mine = query.shape[0]
    eight = pl.pallas_call(
        spread,
        out_shape=jax.ShapeDtypeStruct((8,) + fisher.shape, fisher.dtype),
        in_specs=[pl.BlockSpec(memory_space=pltpu.VMEM)],
        out_specs=pl.BlockSpec(memory_space=pl.ANY),
        scratch_shapes=[pltpu.SemaphoreType.DMA((8,))],
        name="spread",
    )(fisher)
    plane = lax.all_to_all(eight, ("x", "c"), 0, 0)
    plane = plane.reshape(4, -1, k)
    far = lax.ppermute(train, "c", SWAP)
    queries = lax.all_gather(query, "zh", axis=0, tiled=True)
    conditioned = pl.pallas_call(
        condition,
        out_shape=jax.ShapeDtypeStruct((4 * mine, k // 4), jnp.bfloat16),
                compiler_params=pltpu.CompilerParams(vmem_limit_bytes=14 * 2**20),
        cost_estimate=pl.CostEstimate(
            flops=2 * mine * k * k, bytes_accessed=3 * 2**20, transcendentals=0
        ),
        name="condition",
    )(queries, plane)
    conditioned = lax.all_gather(conditioned.reshape(2, 2 * mine, -1), "zh", axis=1)
    conditioned, far = lax.optimization_barrier((conditioned, far))
    first, second = conditioned[0], conditioned[1]
    behind_first, ahead_second = shift_x(first, 1), shift_x(second, -1)
    behind_second, ahead_first = shift_x(second, 1), shift_x(first, -1)
    opposite_first, opposite_second = shift_x(behind_first, 1), shift_x(ahead_second, -1)

    def options(n):
        return dict(
            compiler_params=pltpu.CompilerParams(vmem_limit_bytes=14 * 2**20),
            cost_estimate=pl.CostEstimate(
                flops=8 * n * mine * rows * k, bytes_accessed=6 * 2**20, transcendentals=0
            ),
        )

    own, far = pl.pallas_call(
        score_own,
        out_shape=(
            jax.ShapeDtypeStruct((2, 2, 2, mine, rows), jnp.bfloat16),
            jax.ShapeDtypeStruct((rows, k), jnp.bfloat16),
        ),
        in_specs=[pl.BlockSpec(memory_space=pltpu.VMEM)] * 3 + [pl.BlockSpec(memory_space=pl.ANY)],
        scratch_shapes=[pltpu.SemaphoreType.DMA],
        name="score_own",
        **options(2),
    )(first, second, train, far)
    sides = pl.pallas_call(
        score_sides,
        out_shape=jax.ShapeDtypeStruct((4, 2, 2, mine, rows), jnp.bfloat16),
        name="score_sides",
        **options(4),
    )(behind_first, ahead_second, behind_second, ahead_first, train, far)
    part = pl.pallas_call(
        score_last,
        out_shape=jax.ShapeDtypeStruct((2, 4, 2, 2, mine, rows), jnp.bfloat16),
        name="score_last",
        **options(2),
    )(opposite_first, opposite_second, train, far, own, sides)
    part = lax.all_to_all(part.reshape(16, 2, mine, rows), ("z0", "y", "c"), 0, 0)
    keep, send = pl.pallas_call(
        sum_layers,
        out_shape=(
            jax.ShapeDtypeStruct((2, mine, rows), jnp.float32),
            jax.ShapeDtypeStruct((2, mine, rows), jnp.bfloat16),
        ),
        compiler_params=pltpu.CompilerParams(vmem_limit_bytes=14 * 2**20),
        name="sum_layers",
    )(part.reshape(8, 2, 2, mine, rows))
    total = keep + lax.ppermute(send, "z1", SWAP).astype(jnp.float32)
    return total.reshape(2 * mine, rows).T


def solution(mesh):
    split = Mesh(mesh.devices.reshape(2, 2, 4, 4, 4, 2), LAYER + EX)
    spec = P(LAYER, EX, None)
    return jax.shard_map(
        on_device,
        mesh=split,
        in_specs=(spec, spec, spec),
        out_specs=P(EX, LAYER),
        check_vma=False,
    )
```

```python
import jax
import jax.numpy as jnp
from jax import lax
from jax.experimental import pallas as pl
from jax.experimental.pallas import tpu as pltpu
from jax.sharding import Mesh
from jax.sharding import PartitionSpec as P

LAYER = ("z1", "z0", "y")
EX = ("x", "zh", "c")
SWAP = [(0, 1), (1, 0)]


def copies(block, n):
    return jnp.broadcast_to(block[None], (n,) + block.shape)


def spread(block_ref, out_ref, sem):
    sent = [pltpu.make_async_copy(block_ref, out_ref.at[n], sem.at[n]) for n in range(8)]
    for copy in sent:
        copy.start()
    for copy in sent:
        copy.wait()


def rows_by_rows(a, b):
    return lax.dot_general(
        a, b, (((1,), (1,)), ((), ())), preferred_element_type=jnp.float32
    )


def condition(query_ref, plane_ref, out_ref):
    for x in range(4):
        out = rows_by_rows(query_ref[...], plane_ref[x])
        out_ref[:, x * 128 : x * 128 + 128] = out.astype(jnp.bfloat16)


OWN = ((0, 0), (0, 1))
SIDES = ((3, 0), (1, 1), (3, 1), (1, 0))
OPPOSITE = ((2, 0), (2, 1))


def shift_x(block, by):
    return lax.ppermute(block, "x", [(i, (i + by) % 4) for i in range(4)])


def score(halves, trains, put, arrived=None):
    core = lax.axis_index("c")
    rows, k = trains[0].shape
    thin = k // 16
    for side, train_ref in enumerate(trains):
        if side == 1 and arrived is not None:
            arrived.wait()
        owner = core if side == 0 else 1 - core
        for at in range(0, rows, 256):
            train = train_ref[at : at + 256, :]
            total = None
            for z in range(4):
                columns = [train[:, (x * 4 + z) * thin :][:, :thin] for x in range(4)]
                part = rows_by_rows(
                    jnp.concatenate([half[z] for half in halves], axis=0),
                    jnp.concatenate(columns, axis=1),
                )
                total = part if total is None else total + part
            put(owner, at, total.astype(jnp.bfloat16).reshape(len(halves), 2, -1, 256))


def score_own(first_ref, second_ref, near_ref, far_hbm, out_ref, far_ref, sem):
    arriving = pltpu.make_async_copy(far_hbm, far_ref, sem)
    arriving.start()

    def put(owner, at, block):
        out_ref[:, :, owner, :, at : at + 256] = block

    score((first_ref, second_ref), (near_ref, far_ref), put, arriving)


def score_sides(*refs):
    out_ref = refs[-1]

    def put(owner, at, block):
        out_ref[:, :, owner, :, at : at + 256] = block

    score(refs[:4], refs[4:6], put)


def score_last(first_ref, second_ref, near_ref, far_ref, own_ref, sides_ref, out_ref):
    x = lax.axis_index("x")
    for order, scored in ((OWN, own_ref), (SIDES, sides_ref)):
        for n, (step, half) in enumerate(order):
            at = lax.rem(x + step, 4)
            out_ref[2 * half : 2 * half + 2, :, lax.rem(at, 2), at // 2] = scored[n]

    def put(owner, at, block):
        to = lax.rem(x + 2, 4)
        for n, (_, half) in enumerate(OPPOSITE):
            out_ref[2 * half : 2 * half + 2, owner, lax.rem(to, 2), to // 2, :, at : at + 256] = block[n]

    score((first_ref, second_ref), (near_ref, far_ref), put)


def sum_layers(part_ref, keep_ref, send_ref):
    mine = lax.axis_index("z1")
    for side in range(2):
        for out_ref, z1 in ((keep_ref, mine), (send_ref, 1 - mine)):
            total = jnp.zeros(keep_ref.shape[1:], jnp.float32)
            for n in range(8):
                total += part_ref[n // 2, side, n % 2, z1].astype(jnp.float32)
            out_ref[side] = total.astype(out_ref.dtype)


def on_device(train_grads, query_grads, inverse_fisher):
    train, query, fisher = train_grads[0], query_grads[0], inverse_fisher[0]
    rows, k = train.shape
    mine = query.shape[0]
    eight = pl.pallas_call(
        spread,
        out_shape=jax.ShapeDtypeStruct((8,) + fisher.shape, fisher.dtype),
        in_specs=[pl.BlockSpec(memory_space=pltpu.VMEM)],
        out_specs=pl.BlockSpec(memory_space=pl.ANY),
        scratch_shapes=[pltpu.SemaphoreType.DMA((8,))],
        name="spread",
    )(fisher)
    plane = lax.all_to_all(eight, ("x", "c"), 0, 0)
    plane = plane.reshape(4, -1, k)
    far = lax.ppermute(train, "c", SWAP)
    queries = lax.all_gather(query, "zh", axis=0, tiled=True)
    conditioned = pl.pallas_call(
        condition,
        out_shape=jax.ShapeDtypeStruct((4 * mine, k // 4), jnp.bfloat16),
                compiler_params=pltpu.CompilerParams(vmem_limit_bytes=14 * 2**20),
        cost_estimate=pl.CostEstimate(
            flops=2 * mine * k * k, bytes_accessed=3 * 2**20, transcendentals=0
        ),
        name="condition",
    )(queries, plane)
    conditioned = lax.all_gather(conditioned.reshape(2, 2 * mine, -1), "zh", axis=1)
    conditioned, far = lax.optimization_barrier((conditioned, far))
    first, second = conditioned[0], conditioned[1]
    behind_first, ahead_second = shift_x(first, 1), shift_x(second, -1)
    behind_second, ahead_first = shift_x(second, 1), shift_x(first, -1)
    opposite_first, opposite_second = shift_x(behind_first, 1), shift_x(ahead_second, -1)

    def options(n):
        return dict(
            compiler_params=pltpu.CompilerParams(vmem_limit_bytes=14 * 2**20),
            cost_estimate=pl.CostEstimate(
                flops=8 * n * mine * rows * k, bytes_accessed=6 * 2**20, transcendentals=0
            ),
        )

    own, far = pl.pallas_call(
        score_own,
        out_shape=(
            jax.ShapeDtypeStruct((2, 2, 2, mine, rows), jnp.bfloat16),
            jax.ShapeDtypeStruct((rows, k), jnp.bfloat16),
        ),
        in_specs=[pl.BlockSpec(memory_space=pltpu.VMEM)] * 3 + [pl.BlockSpec(memory_space=pl.ANY)],
        scratch_shapes=[pltpu.SemaphoreType.DMA],
        name="score_own",
        **options(2),
    )(first, second, train, far)
    sides = pl.pallas_call(
        score_sides,
        out_shape=jax.ShapeDtypeStruct((4, 2, 2, mine, rows), jnp.bfloat16),
        name="score_sides",
        **options(4),
    )(behind_first, ahead_second, behind_second, ahead_first, train, far)
    part = pl.pallas_call(
        score_last,
        out_shape=jax.ShapeDtypeStruct((4, 2, 2, 2, mine, rows), jnp.bfloat16),
        name="score_last",
        **options(2),
    )(opposite_first, opposite_second, train, far, own, sides)
    part = lax.all_to_all(part.reshape(16, 2, mine, rows), ("y", "c", "z0"), 0, 0)
    keep, send = pl.pallas_call(
        sum_layers,
        out_shape=(
            jax.ShapeDtypeStruct((2, mine, rows), jnp.float32),
            jax.ShapeDtypeStruct((2, mine, rows), jnp.bfloat16),
        ),
        compiler_params=pltpu.CompilerParams(vmem_limit_bytes=14 * 2**20),
        name="sum_layers",
    )(part.reshape(4, 2, 2, 2, mine, rows))
    total = keep + lax.ppermute(send, "z1", SWAP).astype(jnp.float32)
    return total.reshape(2 * mine, rows).T


def solution(mesh):
    split = Mesh(mesh.devices.reshape(2, 2, 4, 4, 4, 2), LAYER + EX)
    spec = P(LAYER, EX, None)
    return jax.shard_map(
        on_device,
        mesh=split,
        in_specs=(spec, spec, spec),
        out_specs=P(EX, LAYER),
        check_vma=False,
    )
```

```python
import jax
import jax.numpy as jnp
from jax import lax
from jax.experimental import pallas as pl
from jax.experimental.pallas import tpu as pltpu
from jax.sharding import Mesh
from jax.sharding import PartitionSpec as P

LAYER = ("z1", "z0", "y")
EX = ("x", "zh", "c")
SWAP = [(0, 1), (1, 0)]


def copies(block, n):
    return jnp.broadcast_to(block[None], (n,) + block.shape)


def rows_by_rows(a, b):
    return lax.dot_general(
        a, b, (((1,), (1,)), ((), ())), preferred_element_type=jnp.float32
    )


def condition(query_ref, plane_ref, out_ref):
    for x in range(4):
        out = rows_by_rows(query_ref[...], plane_ref[x])
        out_ref[:, x * 128 : x * 128 + 128] = out.astype(jnp.bfloat16)


OWN = ((0, 0), (0, 1))
SIDES = ((3, 0), (1, 1), (3, 1), (1, 0))
OPPOSITE = ((2, 0), (2, 1))


def shift_x(block, by):
    return lax.ppermute(block, "x", [(i, (i + by) % 4) for i in range(4)])


def score(halves, trains, put, arrived=None):
    core = lax.axis_index("c")
    rows, k = trains[0].shape
    thin = k // 16
    for side, train_ref in enumerate(trains):
        if side == 1 and arrived is not None:
            arrived.wait()
        owner = core if side == 0 else 1 - core
        for at in range(0, rows, 256):
            train = train_ref[at : at + 256, :]
            total = None
            for z in range(4):
                columns = [train[:, (x * 4 + z) * thin :][:, :thin] for x in range(4)]
                part = rows_by_rows(
                    jnp.concatenate([half[z] for half in halves], axis=0),
                    jnp.concatenate(columns, axis=1),
                )
                total = part if total is None else total + part
            put(owner, at, total.astype(jnp.bfloat16).reshape(len(halves), 2, -1, 256))


def score_own(first_ref, second_ref, near_ref, far_hbm, out_ref, far_ref, sem):
    arriving = pltpu.make_async_copy(far_hbm, far_ref, sem)
    arriving.start()

    def put(owner, at, block):
        out_ref[:, :, owner, :, at : at + 256] = block

    score((first_ref, second_ref), (near_ref, far_ref), put, arriving)


def score_sides(*refs):
    out_ref = refs[-1]

    def put(owner, at, block):
        out_ref[:, :, owner, :, at : at + 256] = block

    score(refs[:4], refs[4:6], put)


def score_last(first_ref, second_ref, near_ref, far_ref, own_ref, sides_ref, out_ref):
    x = lax.axis_index("x")
    for order, scored in ((OWN, own_ref), (SIDES, sides_ref)):
        for n, (step, half) in enumerate(order):
            at = lax.rem(x + step, 4)
            out_ref[2 * half : 2 * half + 2, :, lax.rem(at, 2), at // 2] = scored[n]

    def put(owner, at, block):
        to = lax.rem(x + 2, 4)
        for n, (_, half) in enumerate(OPPOSITE):
            out_ref[2 * half : 2 * half + 2, owner, lax.rem(to, 2), to // 2, :, at : at + 256] = block[n]

    score((first_ref, second_ref), (near_ref, far_ref), put)


def sum_layers(part_ref, keep_ref, send_ref):
    mine = lax.axis_index("z1")
    for side in range(2):
        for out_ref, z1 in ((keep_ref, mine), (send_ref, 1 - mine)):
            total = jnp.zeros(keep_ref.shape[1:], jnp.float32)
            for n in range(8):
                total += part_ref[n // 2, side, n % 2, z1].astype(jnp.float32)
            out_ref[side] = total.astype(out_ref.dtype)


def on_device(train_grads, query_grads, inverse_fisher):
    train, query, fisher = train_grads[0], query_grads[0], inverse_fisher[0]
    rows, k = train.shape
    mine = query.shape[0]
    plane = lax.all_to_all(copies(fisher, 8), ("x", "c"), 0, 0)
    plane = plane.reshape(4, -1, k)
    far = lax.ppermute(train, "c", SWAP)
    queries = lax.all_gather(query, "zh", axis=0, tiled=True)
    conditioned = pl.pallas_call(
        condition,
        out_shape=jax.ShapeDtypeStruct((4 * mine, k // 4), jnp.bfloat16),
                compiler_params=pltpu.CompilerParams(vmem_limit_bytes=14 * 2**20),
        cost_estimate=pl.CostEstimate(
            flops=2 * mine * k * k, bytes_accessed=3 * 2**20, transcendentals=0
        ),
        name="condition",
    )(queries, plane)
    conditioned = lax.all_gather(conditioned.reshape(2, 2 * mine, -1), "zh", axis=1)
    conditioned, far = lax.optimization_barrier((conditioned, far))
    first, second = conditioned[0], conditioned[1]
    behind_first, ahead_second = shift_x(first, 1), shift_x(second, -1)
    behind_second, ahead_first = shift_x(second, 1), shift_x(first, -1)
    opposite_first, opposite_second = shift_x(behind_first, 1), shift_x(ahead_second, -1)

    def options(n):
        return dict(
            compiler_params=pltpu.CompilerParams(vmem_limit_bytes=14 * 2**20),
            cost_estimate=pl.CostEstimate(
                flops=8 * n * mine * rows * k, bytes_accessed=6 * 2**20, transcendentals=0
            ),
        )

    own, far = pl.pallas_call(
        score_own,
        out_shape=(
            jax.ShapeDtypeStruct((2, 2, 2, mine, rows), jnp.bfloat16),
            jax.ShapeDtypeStruct((rows, k), jnp.bfloat16),
        ),
        in_specs=[pl.BlockSpec(memory_space=pltpu.VMEM)] * 3 + [pl.BlockSpec(memory_space=pl.ANY)],
        scratch_shapes=[pltpu.SemaphoreType.DMA],
        name="score_own",
        **options(2),
    )(first, second, train, far)
    sides = pl.pallas_call(
        score_sides,
        out_shape=jax.ShapeDtypeStruct((4, 2, 2, mine, rows), jnp.bfloat16),
        name="score_sides",
        **options(4),
    )(behind_first, ahead_second, behind_second, ahead_first, train, far)
    part = pl.pallas_call(
        score_last,
        out_shape=jax.ShapeDtypeStruct((4, 2, 2, 2, mine, rows), jnp.bfloat16),
        name="score_last",
        **options(2),
    )(opposite_first, opposite_second, train, far, own, sides)
    part = lax.all_to_all(part.reshape(16, 2, mine, rows), ("y", "c", "z0"), 0, 0)
    keep, send = pl.pallas_call(
        sum_layers,
        out_shape=(
            jax.ShapeDtypeStruct((2, mine, rows), jnp.float32),
            jax.ShapeDtypeStruct((2, mine, rows), jnp.bfloat16),
        ),
        compiler_params=pltpu.CompilerParams(vmem_limit_bytes=14 * 2**20),
        name="sum_layers",
    )(part.reshape(4, 2, 2, 2, mine, rows))
    total = keep + lax.ppermute(send, "z1", SWAP).astype(jnp.float32)
    return total.reshape(2 * mine, rows).T


def solution(mesh):
    split = Mesh(mesh.devices.reshape(2, 2, 4, 4, 4, 2), LAYER + EX)
    spec = P(LAYER, EX, None)
    return jax.shard_map(
        on_device,
        mesh=split,
        in_specs=(spec, spec, spec),
        out_specs=P(EX, LAYER),
        check_vma=False,
    )
```

```python
import jax
import jax.numpy as jnp
from jax import lax
from jax.experimental import pallas as pl
from jax.experimental.pallas import tpu as pltpu
from jax.sharding import Mesh
from jax.sharding import PartitionSpec as P

LAYER = ("z1", "z0", "y")
EX = ("x", "zh", "c")
SWAP = [(0, 1), (1, 0)]


def copies(block, n):
    return jnp.broadcast_to(block[None], (n,) + block.shape)


def rows_by_rows(a, b):
    return lax.dot_general(
        a, b, (((1,), (1,)), ((), ())), preferred_element_type=jnp.float32
    )


def condition(query_ref, plane_ref, out_ref):
    for x in range(4):
        out = rows_by_rows(query_ref[...], plane_ref[x])
        out_ref[:, x * 128 : x * 128 + 128] = out.astype(jnp.bfloat16)


OWN = ((0, 0), (0, 1))
SIDES = ((3, 0), (1, 1), (3, 1), (1, 0))
OPPOSITE = ((2, 0), (2, 1))


def shift_x(block, by):
    return lax.ppermute(block, "x", [(i, (i + by) % 4) for i in range(4)])


def score(halves, trains, put, arrived=None):
    core = lax.axis_index("c")
    rows, k = trains[0].shape
    thin = k // 16
    for side, train_ref in enumerate(trains):
        if side == 1 and arrived is not None:
            arrived.wait()
        owner = core if side == 0 else 1 - core
        for at in range(0, rows, 256):
            train = train_ref[at : at + 256, :]
            total = None
            for z in range(4):
                columns = [train[:, (x * 4 + z) * thin :][:, :thin] for x in range(4)]
                part = rows_by_rows(
                    jnp.concatenate([half[z] for half in halves], axis=0),
                    jnp.concatenate(columns, axis=1),
                )
                total = part if total is None else total + part
            put(owner, at, total.astype(jnp.bfloat16).reshape(len(halves), 2, -1, 256))


def score_own(first_ref, second_ref, near_ref, far_hbm, out_ref, far_ref, sem):
    arriving = pltpu.make_async_copy(far_hbm, far_ref, sem)
    arriving.start()

    def put(owner, at, block):
        out_ref[:, :, owner, :, at : at + 256] = block

    score((first_ref, second_ref), (near_ref, far_ref), put, arriving)


def score_sides(*refs):
    out_ref = refs[-1]

    def put(owner, at, block):
        out_ref[:, :, owner, :, at : at + 256] = block

    score(refs[:4], refs[4:6], put)


def score_last(first_ref, second_ref, near_ref, far_ref, own_ref, sides_ref, out_ref):
    x = lax.axis_index("x")
    for order, scored in ((OWN, own_ref), (SIDES, sides_ref)):
        for n, (step, half) in enumerate(order):
            at = lax.rem(x + step, 4)
            out_ref[2 * half : 2 * half + 2, :, lax.rem(at, 2), at // 2] = scored[n]

    def put(owner, at, block):
        to = lax.rem(x + 2, 4)
        for n, (_, half) in enumerate(OPPOSITE):
            out_ref[2 * half : 2 * half + 2, owner, lax.rem(to, 2), to // 2, :, at : at + 256] = block[n]

    score((first_ref, second_ref), (near_ref, far_ref), put)


def sum_layers(part_ref, keep_ref, send_ref):
    mine = lax.axis_index("z1")
    for side in range(2):
        for out_ref, z1 in ((keep_ref, mine), (send_ref, 1 - mine)):
            total = jnp.zeros(keep_ref.shape[1:], jnp.float32)
            for n in range(8):
                total += part_ref[n // 2, side, n % 2, z1].astype(jnp.float32)
            out_ref[side] = total.astype(out_ref.dtype)


def on_device(train_grads, query_grads, inverse_fisher):
    train, query, fisher = train_grads[0], query_grads[0], inverse_fisher[0]
    rows, k = train.shape
    mine = query.shape[0]
    plane = lax.all_to_all(copies(fisher, 8), ("x", "c"), 0, 0)
    plane = plane.reshape(4, -1, k)
    far = lax.ppermute(train, "c", SWAP)
    queries = lax.all_gather(query, "zh", axis=0, tiled=True)
    conditioned = pl.pallas_call(
        condition,
        out_shape=jax.ShapeDtypeStruct((4 * mine, k // 4), jnp.bfloat16),
                compiler_params=pltpu.CompilerParams(vmem_limit_bytes=14 * 2**20),
        cost_estimate=pl.CostEstimate(
            flops=2 * mine * k * k, bytes_accessed=3 * 2**20, transcendentals=0
        ),
        name="condition",
    )(queries, plane)
    conditioned, far = lax.optimization_barrier((conditioned, far))
    conditioned = lax.all_gather(conditioned.reshape(2, 2 * mine, -1), "zh", axis=1)
    first, second = conditioned[0], conditioned[1]
    behind_first, ahead_second = shift_x(first, 1), shift_x(second, -1)
    behind_second, ahead_first = shift_x(second, 1), shift_x(first, -1)
    opposite_first, opposite_second = shift_x(behind_first, 1), shift_x(ahead_second, -1)

    def options(n):
        return dict(
            compiler_params=pltpu.CompilerParams(vmem_limit_bytes=14 * 2**20),
            cost_estimate=pl.CostEstimate(
                flops=8 * n * mine * rows * k, bytes_accessed=6 * 2**20, transcendentals=0
            ),
        )

    own, far = pl.pallas_call(
        score_own,
        out_shape=(
            jax.ShapeDtypeStruct((2, 2, 2, mine, rows), jnp.bfloat16),
            jax.ShapeDtypeStruct((rows, k), jnp.bfloat16),
        ),
        in_specs=[pl.BlockSpec(memory_space=pltpu.VMEM)] * 3 + [pl.BlockSpec(memory_space=pl.ANY)],
        scratch_shapes=[pltpu.SemaphoreType.DMA],
        name="score_own",
        **options(2),
    )(first, second, train, far)
    sides = pl.pallas_call(
        score_sides,
        out_shape=jax.ShapeDtypeStruct((4, 2, 2, mine, rows), jnp.bfloat16),
        name="score_sides",
        **options(4),
    )(behind_first, ahead_second, behind_second, ahead_first, train, far)
    part = pl.pallas_call(
        score_last,
        out_shape=jax.ShapeDtypeStruct((4, 2, 2, 2, mine, rows), jnp.bfloat16),
        name="score_last",
        **options(2),
    )(opposite_first, opposite_second, train, far, own, sides)
    part = lax.all_to_all(part.reshape(16, 2, mine, rows), ("y", "c", "z0"), 0, 0)
    keep, send = pl.pallas_call(
        sum_layers,
        out_shape=(
            jax.ShapeDtypeStruct((2, mine, rows), jnp.float32),
            jax.ShapeDtypeStruct((2, mine, rows), jnp.bfloat16),
        ),
        compiler_params=pltpu.CompilerParams(vmem_limit_bytes=14 * 2**20),
        name="sum_layers",
    )(part.reshape(4, 2, 2, 2, mine, rows))
    total = keep + lax.ppermute(send, "z1", SWAP).astype(jnp.float32)
    return total.reshape(2 * mine, rows).T


def solution(mesh):
    split = Mesh(mesh.devices.reshape(2, 2, 4, 4, 4, 2), LAYER + EX)
    spec = P(LAYER, EX, None)
    return jax.shard_map(
        on_device,
        mesh=split,
        in_specs=(spec, spec, spec),
        out_specs=P(EX, LAYER),
        check_vma=False,
    )
```
